32 devices in a mesh: gx: 8 (over y, x, core), gy: 4 (over z).
Axes of the slice: x: 2, y: 2, z: 4, core: 2. Of those that a mesh axis runs over, the one named last changes fastest.
Arguments:
- checkpoint: float32 [19, 64, 256, 128], P(None, 'gx', 'gy'), may hold values from 0 to 1, as said below
- fluid: int32 [64, 256, 128], P('gx', 'gy'), may hold values 0 or 1
- adjoint_in: float32 [19, 64, 256, 128], P(None, 'gx', 'gy'), may hold values from -6 to 6
Outputs:
- state: float32 [19, 64, 256, 128], P(None, 'gx', 'gy')
- adjoint: float32 [19, 64, 256, 128], P(None, 'gx', 'gy')
The draws below stay inside these ranges and needn't reach their ends.
Inputs may be any that keep to these rules, and one draw needn't show every extreme that they name: `checkpoint`: positive populations near equilibrium. 1 marks a fluid cell, 0 a solid one.
All inputs are finite; a program needn't handle non-finite values. No bound on the sum of `fluid` on one device may be relied on, other than what follows from the above.
Results may differ from the reference program's by a relative error of at most 0.0003.
Values sent between devices are 32-bit elements; how exact they have to be, the bound alone decides.
A program may use at most 128 MiB of HBM per device.

```python
import jax
import jax.numpy as jnp
import numpy as np
from jax import lax

Q = 19
NZ = 128
STEPS = 3
NX = 64
NY = 256


VELOCITY = [(0, 0, 0), (1, 0, 0), (-1, 0, 0), (0, 1, 0), (0, -1, 0), (0, 0, 1), (0, 0, -1), (1, 1, 0), (-1, -1, 0), (1, -1, 0), (-1, 1, 0), (1, 0, 1), (-1, 0, -1), (1, 0, -1), (-1, 0, 1), (0, 1, 1), (0, -1, -1), (0, 1, -1), (0, -1, 1)]


WEIGHTS = [1.0 / 3.0] + [1.0 / 18.0] * 6 + [1.0 / 36.0] * 12


def draw_checkpoint(key, part):
    key_density = jax.random.fold_in(key, 11)
    key_flow = jax.random.fold_in(key, 12)
    key_noise = jax.random.fold_in(key, 13)
    density = jax.random.uniform(key_density, (NX, NY, NZ), jnp.float32, 0.9, 1.1)
    flow = jax.random.uniform(key_flow, (3, NX, NY, NZ), jnp.float32, -0.08, 0.08)
    noise = jax.random.uniform(key_noise, (19, NX, NY, NZ), jnp.float32, -0.15, 0.15)
    speeds = jnp.array(VELOCITY, jnp.float32)
    along = speeds[:, 0, None, None, None] * flow[0][None] + speeds[:, 1, None, None, None] * flow[1][None] + speeds[:, 2, None, None, None] * flow[2][None]
    weights = jnp.array(WEIGHTS, jnp.float32)[:, None, None, None]
    return (weights * density[None] * (1.0 + 3.0 * along + noise)).astype(jnp.float32)


def with_ends(result, key, least, largest):
    place = [jax.random.randint(jax.random.fold_in(key, axis), (), 0, length) for axis, length in enumerate(result.shape)]
    longest = result.shape.index(max(result.shape))
    neighbour = place[:longest] + [(place[longest] + 1) % result.shape[longest]] + place[longest + 1:]
    return result.at[tuple(place)].set(least).at[tuple(neighbour)].set(largest)


def block_levels(own_key, extent, split, least, largest):
    def one(axis_at, shards_of):
        heights = jax.random.uniform(jax.random.fold_in(jax.random.fold_in(own_key, 6), axis_at), (shards_of,), jnp.float32, least / len(split), largest / len(split))
        return jnp.repeat(jnp.exp(heights), extent[axis_at] // shards_of).reshape((-1,) + (1,) * (len(extent) - axis_at - 1))

    factor_of = one(*split[0])
    for cut in split[1:]:
        factor_of = factor_of * one(*cut)
    return factor_of


def normal_values(key, extent, spread, bound, split=(), dtype=jnp.bfloat16):
    values = jax.random.normal(key, extent, jnp.float32) * spread
    if len(split) > 0:
        values = block_levels(key, extent, split, -0.22, 0.18) * values
    return jnp.clip(values, min=-bound, max=bound).astype(dtype)


def setup_inputs(seed: int = 0) -> dict:
    key_of = jax.random.split(jax.random.key(seed), 4)
    return {
        "checkpoint": draw_checkpoint(jax.random.fold_in(key_of[3], 71), 0),
        "fluid": with_ends((jax.random.randint(key_of[1], (NX, NY, NZ), 0, 10) < 9).astype(jnp.int32), jax.random.fold_in(key_of[1], 1), 0, 1),
        "adjoint_in": normal_values(key_of[2], (Q, NX, NY, NZ), 1.0, 6.0, ((1, 8), (2, 4)), jnp.float32),
    }


VELOCITY = [(0, 0, 0), (1, 0, 0), (-1, 0, 0), (0, 1, 0), (0, -1, 0), (0, 0, 1), (0, 0, -1), (1, 1, 0), (-1, -1, 0), (1, -1, 0), (-1, 1, 0), (1, 0, 1), (-1, 0, -1), (1, 0, -1), (-1, 0, 1), (0, 1, 1), (0, -1, -1), (0, 1, -1), (0, -1, 1)]
WEIGHTS = [1.0 / 3.0] + [1.0 / 18.0] * 6 + [1.0 / 36.0] * 12
OPPOSITE = [0, 2, 1, 4, 3, 6, 5, 8, 7, 10, 9, 12, 11, 14, 13, 16, 15, 18, 17]
RELAXATION = 1.6

def collide(values):
    speeds = jnp.array(VELOCITY, jnp.float32)
    weights = jnp.array(WEIGHTS, jnp.float32)[:, None, None, None]
    density = lax.optimization_barrier(jnp.sum(values, axis=0))
    moment = jnp.einsum('qc,qxyz->cxyz', speeds, values, precision=lax.Precision.HIGHEST)
    flow = moment / density
    along = jnp.einsum('qc,cxyz->qxyz', speeds, flow, precision=lax.Precision.HIGHEST)
    square = lax.optimization_barrier(jnp.sum(flow * flow, axis=0))
    balance = weights * density * (1.0 + 3.0 * along + 4.5 * along * along - 1.5 * square)
    return values - RELAXATION * (values - balance)

def source(plane, speed):
    moved = jnp.roll(plane, (speed[0], speed[1]), (0, 1))
    if speed[2] == 1:
        moved = jnp.concatenate([jnp.zeros_like(moved[:, :, :1]), moved[:, :, :-1]], 2)
    elif speed[2] == -1:
        moved = jnp.concatenate([moved[:, :, 1:], jnp.zeros_like(moved[:, :, :1])], 2)
    return moved

def advance(values, fluid):
    posted = collide(values)
    fluid_float = fluid.astype(jnp.float32)
    read = jnp.stack([source(posted[channel], VELOCITY[channel]) for channel in range(19)])
    open_source = jnp.stack([source(fluid_float, VELOCITY[channel]) for channel in range(19)]) > 0.5
    bounced = posted[np.array(OPPOSITE)]
    inside = jnp.where(open_source, read, bounced)
    return jnp.where(fluid_float[None] > 0.5, inside, values)

def reference(checkpoint, fluid, adjoint_in):
    current = checkpoint
    for step_index in range(STEPS):
        current = advance(current, fluid)
    _, pull_back = jax.vjp(lambda values: advance(values, fluid), current)
    adjoint, = pull_back(adjoint_in)
    return (current, adjoint)
```

```python
import jax
import jax.numpy as jnp
from jax import lax
from jax.experimental import pallas as pl
from jax.experimental.pallas import tpu as pltpu
from jax.sharding import PartitionSpec as P

VELOCITY = [
    (0, 0, 0),
    (1, 0, 0),
    (-1, 0, 0),
    (0, 1, 0),
    (0, -1, 0),
    (0, 0, 1),
    (0, 0, -1),
    (1, 1, 0),
    (-1, -1, 0),
    (1, -1, 0),
    (-1, 1, 0),
    (1, 0, 1),
    (-1, 0, -1),
    (1, 0, -1),
    (-1, 0, 1),
    (0, 1, 1),
    (0, -1, -1),
    (0, 1, -1),
    (0, -1, 1),
]
OPPOSITE = [0, 2, 1, 4, 3, 6, 5, 8, 7, 10, 9, 12, 11, 14, 13, 16, 15, 18, 17]
ORDER = [0, 1, 7, 9, 11, 13, 2, 8, 10, 12, 14, 3, 4, 5, 6, 15, 16, 17, 18]
SLOT = [ORDER.index(q) for q in range(19)]
UP = [3, 7, 10, 15, 17]
DOWN = [4, 8, 9, 16, 18]
CORNER = [7, 8, 9, 10]
PAD = 8
T = 8
MIB = 1 << 20


def shifted(ref, q, x, y, speed):
    row = PAD + T * y - speed[1]
    tile = ref[SLOT[q], x + 1 - speed[0], row : row + T, :]
    if speed[2]:
        tile = pltpu.roll(tile, speed[2] % tile.shape[1], 1)
    return tile


def own(ref, q, x, y):
    return ref[SLOT[q], x + 1, PAD + T * y : PAD + T * y + T, :]


def stream(ref, bits, x, y):
    result = [own(ref, 0, x, y)]
    for q in range(1, 19):
        is_open = (bits & (1 << q)) != 0
        result.append(
            jnp.where(is_open, shifted(ref, q, x, y, VELOCITY[q]), own(ref, OPPOSITE[q], x, y))
        )
    return result


def moments(v):
    s = {q: v[q] + v[q + 1] for q in range(1, 19, 2)}
    d = {q: v[q] - v[q + 1] for q in range(1, 19, 2)}
    rho = v[0] + ((s[1] + s[3]) + (s[5] + s[7])) + ((s[9] + s[11]) + (s[13] + (s[15] + s[17])))
    mx = d[1] + (d[7] + d[9]) + (d[11] + d[13])
    my = d[3] + (d[7] - d[9]) + (d[15] + d[17])
    mz = d[5] + (d[11] - d[13]) + (d[15] - d[17])
    return rho, mx, my, mz


def collide(v):
    rho, mx, my, mz = moments(v)
    inverse = 3.0 / rho
    ux, uy, uz = mx * inverse, my * inverse, mz * inverse
    base = 1.0 - (ux * ux + uy * uy + uz * uz) * (1.0 / 6.0)
    along = {
        1: ux,
        3: uy,
        5: uz,
        7: ux + uy,
        9: ux - uy,
        11: ux + uz,
        13: ux - uz,
        15: uy + uz,
        17: uy - uz,
    }
    axis, diagonal = rho * (1.6 / 18.0), rho * (1.6 / 36.0)
    result = [rho * (1.6 / 3.0) * base - 0.6 * v[0]]
    for q in range(1, 19, 2):
        a = along[q]
        even = base + 0.5 * (a * a)
        factor = axis if q < 7 else diagonal
        result.append(factor * (even + a) - 0.6 * v[q])
        result.append(factor * (even - a) - 0.6 * v[q + 1])
    return result


def pull_back(v, b):
    rho, mx, my, mz = moments(v)
    inverse = 1.0 / rho
    ux, uy, uz = mx * inverse, my * inverse, mz * inverse
    s = {q: b[q] + b[q + 1] for q in range(1, 19, 2)}
    d = {q: b[q] - b[q + 1] for q in range(1, 19, 2)}
    for q in (1, 3, 5):
        s[q] = s[q] + s[q]
        d[q] = d[q] + d[q]
    sxy_p, sxz_p, syz_p = s[7] + s[9], s[11] + s[13], s[15] + s[17]
    sxy, sxz, syz = s[7] - s[9], s[11] - s[13], s[15] - s[17]
    s0 = 12.0 * b[0] + (s[1] + s[3]) + (s[5] + sxy_p) + (sxz_p + syz_p)
    sxx, syy, szz = s[1] + sxy_p + sxz_p, s[3] + sxy_p + syz_p, s[5] + sxz_p + syz_p
    s1x = d[1] + (d[7] + d[9]) + (d[11] + d[13])
    s1y = d[3] + (d[7] - d[9]) + (d[15] + d[17])
    s1z = d[5] + (d[11] - d[13]) + (d[15] - d[17])
    tx = sxx * ux + sxy * uy + sxz * uz
    ty = sxy * ux + syy * uy + syz * uz
    tz = sxz * ux + syz * uy + szz * uz
    k = 1.6 / 36.0
    square = ux * ux + uy * uy + uz * uz
    level = k * (s0 * (1.0 + 1.5 * square) - 4.5 * (ux * tx + uy * ty + uz * tz))
    gx = (3.0 * k) * (s1x + 3.0 * tx - ux * s0)
    gy = (3.0 * k) * (s1y + 3.0 * ty - uy * s0)
    gz = (3.0 * k) * (s1z + 3.0 * tz - uz * s0)
    along = {
        1: gx,
        3: gy,
        5: gz,
        7: gx + gy,
        9: gx - gy,
        11: gx + gz,
        13: gx - gz,
        15: gy + gz,
        17: gy - gz,
    }
    result = [level - 0.6 * b[0]]
    for q in range(1, 19, 2):
        result.append((level + along[q]) - 0.6 * b[q])
        result.append((level - along[q]) - 0.6 * b[q + 1])
    return result


def forward_kernel(
    start_ref, fluid_ref, seed_ref,
    post_a, held, bits_ref,
    post_b, start, cells, solid, y_send, y_recv, c_send, c_recv,
    load_sem, send_sem, recv_sem,
):
    _, nx, ny, nz = start_ref.shape
    tiles = ny // T
    last = tiles - 1
    top = PAD + ny
    me = {"gx": lax.axis_index("gx"), "gy": lax.axis_index("gy")}
    count = {"gx": lax.axis_size("gx"), "gy": lax.axis_size("gy")}

    def device(dx, dy):
        to_x = lax.rem(me["gx"] + dx + count["gx"], count["gx"])
        to_y = lax.rem(me["gy"] + dy + count["gy"], count["gy"])
        return (to_x, to_y)

    around = [(i, j) for i in (-1, 0, 1) for j in (-1, 0, 1) if (i, j) != (0, 0)]
    barrier = pltpu.get_barrier_semaphore()

    fluid_load = pltpu.make_async_copy(fluid_ref, cells, load_sem.at[0])
    fluid_load.start()
    start_load = [
        pltpu.make_async_copy(start_ref.at[:, pl.ds(a, n)], start.at[:, pl.ds(a, n)], load_sem.at[1 + i])
        for i, (a, n) in enumerate(((0, 1), (nx - 1, 1), (1, nx - 2)))
    ]
    for load in start_load:
        load.start()
    seed_load = [
        pltpu.make_async_copy(
            seed_ref.at[q],
            held.at[SLOT[OPPOSITE[q]], pl.ds(1, nx), pl.ds(PAD, ny)],
            load_sem.at[4 + q],
        )
        for q in range(19)
    ]
    for load in seed_load:
        load.start()
    for i, j in around:
        pl.semaphore_signal(barrier, inc=1, device_id=device(i, j), device_id_type=pl.DeviceIdType.MESH)

    def copies(e, ref, is_cells):
        made = []
        for i, (plane, halo, first) in enumerate(((nx, 0, 1), (1, nx + 1, 6))):
            rows = pl.ds(PAD, ny)
            if is_cells:
                source, target = ref.at[plane, rows], ref.at[halo, rows]
            else:
                five = pl.ds(first, 5)
                source, target = ref.at[five, plane, rows], ref.at[five, halo, rows]
            made.append((source, target, device(1 - 2 * i, 0)))
        for i in range(2):
            made.append((y_send.at[e, i], y_recv.at[e, i], device(0, 1 - 2 * i)))
        for i, q in enumerate(CORNER):
            made.append((c_send.at[e, i], c_recv.at[e, i], device(VELOCITY[q][0], VELOCITY[q][1])))
        return [
            pltpu.make_async_remote_copy(
                src_ref=source, dst_ref=target, send_sem=send_sem.at[e, i], recv_sem=recv_sem.at[e, i],
                device_id=to, device_id_type=pl.DeviceIdType.MESH,
            )
            for i, (source, target, to) in enumerate(made)
        ]

    def pack(e, ref):
        def one(x, _):
            for k in range(5):
                y_send[e, 0, k, x] = ref[SLOT[UP[k]], x + 1, top - 1 : top, :]
                y_send[e, 1, k, x] = ref[SLOT[DOWN[k]], x + 1, PAD : PAD + 1, :]
            return 0

        lax.fori_loop(0, nx, one, 0)
        for i, q in enumerate(CORNER):
            plane = nx if VELOCITY[q][0] == 1 else 1
            row = top - 1 if VELOCITY[q][1] == 1 else PAD
            c_send[e, i] = ref[SLOT[q], plane, row : row + 1, :]

    def unpack(e, ref):
        def one(x, _):
            for k in range(5):
                ref[SLOT[UP[k]], x + 1, PAD - 1 : PAD, :] = y_recv[e, 0, k, x]
                ref[SLOT[DOWN[k]], x + 1, top : top + 1, :] = y_recv[e, 1, k, x]
            return 0

        lax.fori_loop(0, nx, one, 0)
        for i, q in enumerate(CORNER):
            plane = 0 if VELOCITY[q][0] == 1 else nx + 1
            row = PAD - 1 if VELOCITY[q][1] == 1 else top
            ref[SLOT[q], plane, row : row + 1, :] = c_recv[e, i]

    def sweep_rim(body):
        def face(i, _):
            for y in range(tiles):
                body(i * (nx - 1), y)
            return 0

        def edge(x, _):
            body(x, 0)
            body(x, last)
            return 0

        lax.fori_loop(0, 2, face, 0)
        lax.fori_loop(1, nx - 1, edge, 0)

    def sweep_interior(body):
        def line(x, _):
            for y in range(1, last):
                body(x, y)
            return 0

        lax.fori_loop(1, nx - 1, line, 0)

    def begin(made):
        for copy in made:
            copy.start()

    def finish(made):
        for copy in made:
            copy.wait()

    fluid_load.wait()

    def to_float(x, _):
        solid[x + 1, PAD:top, :] = cells[x].astype(jnp.float32)
        y_send[0, 0, 0, x] = solid[x + 1, top - 1 : top, :]
        y_send[0, 1, 0, x] = solid[x + 1, PAD : PAD + 1, :]
        for k in range(1, 5):
            y_send[0, 0, k, x] = jnp.zeros((1, nz), jnp.float32)
            y_send[0, 1, k, x] = jnp.zeros((1, nz), jnp.float32)
        return 0

    lax.fori_loop(0, nx, to_float, 0)
    for i, q in enumerate(CORNER):
        plane = nx if VELOCITY[q][0] == 1 else 1
        row = top - 1 if VELOCITY[q][1] == 1 else PAD
        c_send[0, i] = solid[plane, row : row + 1, :]
    pl.semaphore_wait(barrier, len(around))
    cell_copies = copies(0, solid, True)
    begin(cell_copies)

    def store(to, x, y, v, is_fluid):
        for q, value in enumerate(collide(v)):
            to[SLOT[q], x + 1, PAD + T * y : PAD + T * y + T, :] = jnp.where(
                is_fluid, value, v[OPPOSITE[q]]
            )

    def first(x, y):
        v = [start[q, x, T * y : T * y + T, :] for q in range(19)]
        store(post_a, x, y, v, solid[x + 1, PAD + T * y : PAD + T * y + T, :] > 0.5)

    for load in start_load:
        load.wait()
    sweep_rim(first)
    pack(1, post_a)
    first_copies = copies(1, post_a, False)
    begin(first_copies)
    sweep_interior(first)

    for load in seed_load:
        load.wait()
    pack(4, held)
    seed_copies = copies(4, held, False)
    begin(seed_copies)

    finish(cell_copies)

    def place_cells(x, _):
        solid[x + 1, PAD - 1 : PAD, :] = y_recv[0, 0, 0, x]
        solid[x + 1, top : top + 1, :] = y_recv[0, 1, 0, x]
        return 0

    lax.fori_loop(0, nx, place_cells, 0)
    for i, q in enumerate(CORNER):
        plane = 0 if VELOCITY[q][0] == 1 else nx + 1
        row = PAD - 1 if VELOCITY[q][1] == 1 else top
        solid[plane, row : row + 1, :] = c_recv[0, i]

    layer = lax.broadcasted_iota(jnp.int32, (T, nz), 1)
    inside = {1: (layer > 0).astype(jnp.float32), -1: (layer < nz - 1).astype(jnp.float32)}

    def mark(x, _):
        for y in range(tiles):
            flat, up, down = 1.0, 0.0, 0.0
            for q in range(1, 19):
                c = VELOCITY[q]
                row = PAD + T * y - c[1]
                tile = solid[x + 1 - c[0], row : row + T, :] * float(1 << q)
                if c[2] == 0:
                    flat = flat + tile
                elif c[2] == 1:
                    up = up + tile
                else:
                    down = down + tile
            total = flat + pltpu.roll(up, 1, 1) * inside[1] + pltpu.roll(down, nz - 1, 1) * inside[-1]
            here = solid[x + 1, PAD + T * y : PAD + T * y + T, :]
            bits_ref[x, T * y : T * y + T, :] = (total * here).astype(jnp.int32)
        return 0

    lax.fori_loop(0, nx, mark, 0)

    def middle(source, to):
        def body(x, y):
            bits = bits_ref[x, T * y : T * y + T, :]
            v = stream(source, bits, x, y)
            store(to, x, y, v, (bits & 1) != 0)

        return body

    sweep_interior(middle(post_a, post_b))
    finish(first_copies)
    unpack(1, post_a)
    sweep_rim(middle(post_a, post_b))
    pack(2, post_b)
    second_copies = copies(2, post_b, False)
    begin(second_copies)
    sweep_interior(middle(post_b, post_a))
    finish(second_copies)
    unpack(2, post_b)
    sweep_rim(middle(post_b, post_a))
    pack(3, post_a)
    third_copies = copies(3, post_a, False)
    begin(third_copies)
    finish(seed_copies)
    unpack(4, held)
    finish(third_copies)
    unpack(3, post_a)


def adjoint_kernel(post, held, bits_ref, state_ref, adjoint_ref):
    x = pl.program_id(0)
    tiles = bits_ref.shape[1] // T
    for y in range(tiles):
        rows = slice(T * y, T * y + T)
        bits = bits_ref[x, rows, :]
        v = stream(post, bits, x, y)
        for q in range(19):
            state_ref[q, 0, rows, :] = v[q]
        turned = stream(held, bits, x, y)
        b = [turned[OPPOSITE[q]] for q in range(19)]
        through = pull_back(v, b)
        is_fluid = (bits & 1) != 0
        for q in range(19):
            adjoint_ref[q, 0, rows, :] = jnp.where(is_fluid, through[q], turned[q])


def per_device(checkpoint, fluid, adjoint_in):
    n, nx, ny, nz = checkpoint.shape
    padded = (n, nx + 2, ny + 2 * PAD, nz)
    f32 = jnp.float32
    post, held, bits = pl.pallas_call(
        forward_kernel,
        out_shape=(
            pltpu.VMEM(padded, f32),
            pltpu.VMEM(padded, f32),
            pltpu.VMEM((nx, ny, nz), jnp.int32),
        ),
        in_specs=[pl.BlockSpec(memory_space=pl.ANY)] * 3,
        out_specs=[pl.BlockSpec(memory_space=pltpu.VMEM)] * 3,
        scratch_shapes=[
            pltpu.VMEM(padded, f32),
            pltpu.VMEM((n, nx, ny, nz), f32),
            pltpu.VMEM((nx, ny, nz), jnp.int32),
            pltpu.VMEM(padded[1:], f32),
            pltpu.VMEM((5, 2, 5, nx, 1, nz), f32),
            pltpu.VMEM((5, 2, 5, nx, 1, nz), f32),
            pltpu.VMEM((5, 4, 1, nz), f32),
            pltpu.VMEM((5, 4, 1, nz), f32),
            pltpu.SemaphoreType.DMA((23,)),
            pltpu.SemaphoreType.DMA((5, 8)),
            pltpu.SemaphoreType.DMA((5, 8)),
        ],
        compiler_params=pltpu.CompilerParams(
            collective_id=0, has_side_effects=True, vmem_limit_bytes=40 * MIB
        ),
        name="forward",
    )(checkpoint, fluid, adjoint_in)
    block = pl.BlockSpec((n, 1, ny, nz), lambda x: (0, x, 0, 0))
    return pl.pallas_call(
        adjoint_kernel,
        grid=(nx,),
        out_shape=(jax.ShapeDtypeStruct((n, nx, ny, nz), f32),) * 2,
        in_specs=[pl.BlockSpec(memory_space=pltpu.VMEM)] * 3,
        out_specs=(block, block),
        compiler_params=pltpu.CompilerParams(vmem_limit_bytes=12 * MIB),
        name="adjoint",
    )(post, held, bits)


def solution(mesh):
    return jax.shard_map(
        per_device,
        mesh=mesh,
        in_specs=(P(None, "gx", "gy", None), P("gx", "gy", None), P(None, "gx", "gy", None)),
        out_specs=(P(None, "gx", "gy", None), P(None, "gx", "gy", None)),
        check_vma=False,
    )
```

```python
import jax
import jax.numpy as jnp
from jax import lax
from jax.experimental import pallas as pl
from jax.experimental.pallas import tpu as pltpu
from jax.sharding import PartitionSpec as P

VELOCITY = [
    (0, 0, 0),
    (1, 0, 0),
    (-1, 0, 0),
    (0, 1, 0),
    (0, -1, 0),
    (0, 0, 1),
    (0, 0, -1),
    (1, 1, 0),
    (-1, -1, 0),
    (1, -1, 0),
    (-1, 1, 0),
    (1, 0, 1),
    (-1, 0, -1),
    (1, 0, -1),
    (-1, 0, 1),
    (0, 1, 1),
    (0, -1, -1),
    (0, 1, -1),
    (0, -1, 1),
]
OPPOSITE = [0, 2, 1, 4, 3, 6, 5, 8, 7, 10, 9, 12, 11, 14, 13, 16, 15, 18, 17]
ORDER = [0, 1, 7, 9, 11, 13, 2, 8, 10, 12, 14, 3, 4, 5, 6, 15, 16, 17, 18]
SLOT = [ORDER.index(q) for q in range(19)]
UP = [3, 7, 10, 15, 17]
DOWN = [4, 8, 9, 16, 18]
CORNER = [7, 8, 9, 10]
PAD = 8
T = 8
MIB = 1 << 20


def shifted(ref, q, x, y, speed):
    row = PAD + T * y - speed[1]
    tile = ref[SLOT[q], x + 1 - speed[0], row : row + T, :]
    if speed[2]:
        tile = pltpu.roll(tile, speed[2] % tile.shape[1], 1)
    return tile


def own(ref, q, x, y):
    return ref[SLOT[q], x + 1, PAD + T * y : PAD + T * y + T, :]


def stream(ref, bits, x, y):
    result = [own(ref, 0, x, y)]
    for q in range(1, 19):
        is_open = (bits & (1 << q)) != 0
        result.append(
            jnp.where(is_open, shifted(ref, q, x, y, VELOCITY[q]), own(ref, OPPOSITE[q], x, y))
        )
    return result


def moments(v):
    s = {q: v[q] + v[q + 1] for q in range(1, 19, 2)}
    d = {q: v[q] - v[q + 1] for q in range(1, 19, 2)}
    rho = v[0] + ((s[1] + s[3]) + (s[5] + s[7])) + ((s[9] + s[11]) + (s[13] + (s[15] + s[17])))
    mx = d[1] + (d[7] + d[9]) + (d[11] + d[13])
    my = d[3] + (d[7] - d[9]) + (d[15] + d[17])
    mz = d[5] + (d[11] - d[13]) + (d[15] - d[17])
    return rho, mx, my, mz


def collide(v):
    rho, mx, my, mz = moments(v)
    inverse = 3.0 / rho
    ux, uy, uz = mx * inverse, my * inverse, mz * inverse
    base = 1.0 - (ux * ux + uy * uy + uz * uz) * (1.0 / 6.0)
    along = {
        1: ux,
        3: uy,
        5: uz,
        7: ux + uy,
        9: ux - uy,
        11: ux + uz,
        13: ux - uz,
        15: uy + uz,
        17: uy - uz,
    }
    axis, diagonal = rho * (1.6 / 18.0), rho * (1.6 / 36.0)
    result = [rho * (1.6 / 3.0) * base - 0.6 * v[0]]
    for q in range(1, 19, 2):
        a = along[q]
        even = base + 0.5 * (a * a)
        factor = axis if q < 7 else diagonal
        result.append(factor * (even + a) - 0.6 * v[q])
        result.append(factor * (even - a) - 0.6 * v[q + 1])
    return result


def pull_back(v, b):
    rho, mx, my, mz = moments(v)
    inverse = 1.0 / rho
    ux, uy, uz = mx * inverse, my * inverse, mz * inverse
    s = {q: b[q] + b[q + 1] for q in range(1, 19, 2)}
    d = {q: b[q] - b[q + 1] for q in range(1, 19, 2)}
    for q in (1, 3, 5):
        s[q] = s[q] + s[q]
        d[q] = d[q] + d[q]
    sxy_p, sxz_p, syz_p = s[7] + s[9], s[11] + s[13], s[15] + s[17]
    sxy, sxz, syz = s[7] - s[9], s[11] - s[13], s[15] - s[17]
    s0 = 12.0 * b[0] + (s[1] + s[3]) + (s[5] + sxy_p) + (sxz_p + syz_p)
    sxx, syy, szz = s[1] + sxy_p + sxz_p, s[3] + sxy_p + syz_p, s[5] + sxz_p + syz_p
    s1x = d[1] + (d[7] + d[9]) + (d[11] + d[13])
    s1y = d[3] + (d[7] - d[9]) + (d[15] + d[17])
    s1z = d[5] + (d[11] - d[13]) + (d[15] - d[17])
    tx = sxx * ux + sxy * uy + sxz * uz
    ty = sxy * ux + syy * uy + syz * uz
    tz = sxz * ux + syz * uy + szz * uz
    k = 1.6 / 36.0
    square = ux * ux + uy * uy + uz * uz
    level = k * (s0 * (1.0 + 1.5 * square) - 4.5 * (ux * tx + uy * ty + uz * tz))
    gx = (3.0 * k) * (s1x + 3.0 * tx - ux * s0)
    gy = (3.0 * k) * (s1y + 3.0 * ty - uy * s0)
    gz = (3.0 * k) * (s1z + 3.0 * tz - uz * s0)
    along = {
        1: gx,
        3: gy,
        5: gz,
        7: gx + gy,
        9: gx - gy,
        11: gx + gz,
        13: gx - gz,
        15: gy + gz,
        17: gy - gz,
    }
    result = [level - 0.6 * b[0]]
    for q in range(1, 19, 2):
        result.append((level + along[q]) - 0.6 * b[q])
        result.append((level - along[q]) - 0.6 * b[q + 1])
    return result


def forward_kernel(
    start_ref, fluid_ref, seed_ref,
    state_ref, adjoint_ref,
    post_a, held, bits_ref, post_b, start, cells, solid, y_send, y_recv, c_send, c_recv,
    load_sem, send_sem, recv_sem,
):
    _, nx, ny, nz = start_ref.shape
    tiles = ny // T
    last = tiles - 1
    top = PAD + ny
    me = {"gx": lax.axis_index("gx"), "gy": lax.axis_index("gy")}
    count = {"gx": lax.axis_size("gx"), "gy": lax.axis_size("gy")}

    def device(dx, dy):
        to_x = lax.rem(me["gx"] + dx + count["gx"], count["gx"])
        to_y = lax.rem(me["gy"] + dy + count["gy"], count["gy"])
        return (to_x, to_y)

    around = [(i, j) for i in (-1, 0, 1) for j in (-1, 0, 1) if (i, j) != (0, 0)]
    barrier = pltpu.get_barrier_semaphore()

    fluid_load = pltpu.make_async_copy(fluid_ref, cells, load_sem.at[0])
    fluid_load.start()
    start_load = [
        pltpu.make_async_copy(start_ref.at[:, pl.ds(a, n)], start.at[:, pl.ds(a, n)], load_sem.at[1 + i])
        for i, (a, n) in enumerate(((0, 1), (nx - 1, 1), (1, nx - 2)))
    ]
    for load in start_load:
        load.start()
    seed_load = [
        pltpu.make_async_copy(
            seed_ref.at[q],
            held.at[SLOT[OPPOSITE[q]], pl.ds(1, nx), pl.ds(PAD, ny)],
            load_sem.at[4 + q],
        )
        for q in range(19)
    ]
    for i, j in around:
        pl.semaphore_signal(barrier, inc=1, device_id=device(i, j), device_id_type=pl.DeviceIdType.MESH)

    def copies(e, ref, is_cells):
        made = []
        for i, (plane, halo, first) in enumerate(((nx, 0, 1), (1, nx + 1, 6))):
            rows = pl.ds(PAD, ny)
            if is_cells:
                source, target = ref.at[plane, rows], ref.at[halo, rows]
            else:
                five = pl.ds(first, 5)
                source, target = ref.at[five, plane, rows], ref.at[five, halo, rows]
            made.append((source, target, device(1 - 2 * i, 0)))
        for i in range(2):
            made.append((y_send.at[e, i], y_recv.at[e, i], device(0, 1 - 2 * i)))
        for i, q in enumerate(CORNER):
            made.append((c_send.at[e, i], c_recv.at[e, i], device(VELOCITY[q][0], VELOCITY[q][1])))
        return [
            pltpu.make_async_remote_copy(
                src_ref=source, dst_ref=target, send_sem=send_sem.at[e, i], recv_sem=recv_sem.at[e, i],
                device_id=to, device_id_type=pl.DeviceIdType.MESH,
            )
            for i, (source, target, to) in enumerate(made)
        ]

    def pack(e, ref):
        def one(x, _):
            for k in range(5):
                y_send[e, 0, k, x] = ref[SLOT[UP[k]], x + 1, top - 1 : top, :]
                y_send[e, 1, k, x] = ref[SLOT[DOWN[k]], x + 1, PAD : PAD + 1, :]
            return 0

        lax.fori_loop(0, nx, one, 0)
        for i, q in enumerate(CORNER):
            plane = nx if VELOCITY[q][0] == 1 else 1
            row = top - 1 if VELOCITY[q][1] == 1 else PAD
            c_send[e, i] = ref[SLOT[q], plane, row : row + 1, :]

    def unpack(e, ref):
        def one(x, _):
            for k in range(5):
                ref[SLOT[UP[k]], x + 1, PAD - 1 : PAD, :] = y_recv[e, 0, k, x]
                ref[SLOT[DOWN[k]], x + 1, top : top + 1, :] = y_recv[e, 1, k, x]
            return 0

        lax.fori_loop(0, nx, one, 0)
        for i, q in enumerate(CORNER):
            plane = 0 if VELOCITY[q][0] == 1 else nx + 1
            row = PAD - 1 if VELOCITY[q][1] == 1 else top
            ref[SLOT[q], plane, row : row + 1, :] = c_recv[e, i]

    def sweep_rim(body):
        def face(i, _):
            for y in range(tiles):
                body(i * (nx - 1), y)
            return 0

        def edge(x, _):
            body(x, 0)
            body(x, last)
            return 0

        lax.fori_loop(0, 2, face, 0)
        lax.fori_loop(1, nx - 1, edge, 0)

    def sweep_interior(body):
        def line(x, _):
            for y in range(1, last):
                body(x, y)
            return 0

        lax.fori_loop(1, nx - 1, line, 0)

    def begin(made):
        for copy in made:
            copy.start()

    def finish(made):
        for copy in made:
            copy.wait()

    fluid_load.wait()

    def to_float(x, _):
        solid[x + 1, PAD:top, :] = cells[x].astype(jnp.float32)
        y_send[0, 0, 0, x] = solid[x + 1, top - 1 : top, :]
        y_send[0, 1, 0, x] = solid[x + 1, PAD : PAD + 1, :]
        for k in range(1, 5):
            y_send[0, 0, k, x] = jnp.zeros((1, nz), jnp.float32)
            y_send[0, 1, k, x] = jnp.zeros((1, nz), jnp.float32)
        return 0

    lax.fori_loop(0, nx, to_float, 0)
    for i, q in enumerate(CORNER):
        plane = nx if VELOCITY[q][0] == 1 else 1
        row = top - 1 if VELOCITY[q][1] == 1 else PAD
        c_send[0, i] = solid[plane, row : row + 1, :]
    pl.semaphore_wait(barrier, len(around))
    cell_copies = copies(0, solid, True)
    begin(cell_copies)

    def store(to, x, y, v, is_fluid):
        for q, value in enumerate(collide(v)):
            to[SLOT[q], x + 1, PAD + T * y : PAD + T * y + T, :] = jnp.where(
                is_fluid, value, v[OPPOSITE[q]]
            )

    def first(x, y):
        v = [start[q, x, T * y : T * y + T, :] for q in range(19)]
        store(post_a, x, y, v, solid[x + 1, PAD + T * y : PAD + T * y + T, :] > 0.5)

    for load in start_load:
        load.wait()
    for load in seed_load:
        load.start()
    sweep_rim(first)
    pack(1, post_a)
    first_copies = copies(1, post_a, False)
    begin(first_copies)
    sweep_interior(first)

    for load in seed_load:
        load.wait()
    pack(4, held)
    seed_copies = copies(4, held, False)
    begin(seed_copies)

    finish(cell_copies)

    def place_cells(x, _):
        solid[x + 1, PAD - 1 : PAD, :] = y_recv[0, 0, 0, x]
        solid[x + 1, top : top + 1, :] = y_recv[0, 1, 0, x]
        return 0

    lax.fori_loop(0, nx, place_cells, 0)
    for i, q in enumerate(CORNER):
        plane = 0 if VELOCITY[q][0] == 1 else nx + 1
        row = PAD - 1 if VELOCITY[q][1] == 1 else top
        solid[plane, row : row + 1, :] = c_recv[0, i]

    layer = lax.broadcasted_iota(jnp.int32, (T, nz), 1)
    inside = {1: (layer > 0).astype(jnp.float32), -1: (layer < nz - 1).astype(jnp.float32)}

    def mark(x, _):
        for y in range(tiles):
            flat, up, down = 1.0, 0.0, 0.0
            for q in range(1, 19):
                c = VELOCITY[q]
                row = PAD + T * y - c[1]
                tile = solid[x + 1 - c[0], row : row + T, :] * float(1 << q)
                if c[2] == 0:
                    flat = flat + tile
                elif c[2] == 1:
                    up = up + tile
                else:
                    down = down + tile
            total = flat + pltpu.roll(up, 1, 1) * inside[1] + pltpu.roll(down, nz - 1, 1) * inside[-1]
            here = solid[x + 1, PAD + T * y : PAD + T * y + T, :]
            bits_ref[x, T * y : T * y + T, :] = (total * here).astype(jnp.int32)
        return 0

    lax.fori_loop(0, nx, mark, 0)

    def middle(source, to):
        def body(x, y):
            bits = bits_ref[x, T * y : T * y + T, :]
            v = stream(source, bits, x, y)
            store(to, x, y, v, (bits & 1) != 0)

        return body

    sweep_interior(middle(post_a, post_b))
    finish(first_copies)
    unpack(1, post_a)
    sweep_rim(middle(post_a, post_b))
    pack(2, post_b)
    second_copies = copies(2, post_b, False)
    begin(second_copies)
    sweep_interior(middle(post_b, post_a))
    finish(second_copies)
    unpack(2, post_b)
    sweep_rim(middle(post_b, post_a))
    pack(3, post_a)
    third_copies = copies(3, post_a, False)
    begin(third_copies)
    finish(seed_copies)
    unpack(4, held)

    def final(x, y):
        rows = slice(T * y, T * y + T)
        bits = bits_ref[x, rows, :]
        v = stream(post_a, bits, x, y)
        for q in range(19):
            state_ref[q, x, rows, :] = v[q]
        turned = stream(held, bits, x, y)
        through = pull_back(v, [turned[OPPOSITE[q]] for q in range(19)])
        is_fluid = (bits & 1) != 0
        for q in range(19):
            adjoint_ref[q, x, rows, :] = jnp.where(is_fluid, through[q], turned[q])

    sweep_interior(final)
    finish(third_copies)
    unpack(3, post_a)
    sweep_rim(final)


def write_kernel(state_in, adjoint_in, state_ref, adjoint_ref, sem):
    made = []
    for i, (source, target) in enumerate(((state_in, state_ref), (adjoint_in, adjoint_ref))):
        for q in range(source.shape[0]):
            made.append(pltpu.make_async_copy(source.at[q], target.at[q], sem.at[i, q]))
    for copy in made:
        copy.start()
    for copy in made:
        copy.wait()


def per_device(checkpoint, fluid, adjoint_in):
    n, nx, ny, nz = checkpoint.shape
    padded = (n, nx + 2, ny + 2 * PAD, nz)
    f32 = jnp.float32
    state, adjoint = pl.pallas_call(
        forward_kernel,
        out_shape=(
            pltpu.VMEM((n, nx, ny, nz), f32),
            pltpu.VMEM((n, nx, ny, nz), f32),
        ),
        in_specs=[pl.BlockSpec(memory_space=pltpu.HBM)] * 3,
        out_specs=[pl.BlockSpec(memory_space=pltpu.VMEM)] * 2,
        scratch_shapes=[
            pltpu.VMEM(padded, f32),
            pltpu.VMEM(padded, f32),
            pltpu.VMEM((nx, ny, nz), jnp.int32),
            pltpu.VMEM(padded, f32),
            pltpu.VMEM((n, nx, ny, nz), f32),
            pltpu.VMEM((nx, ny, nz), jnp.int32),
            pltpu.VMEM(padded[1:], f32),
            pltpu.VMEM((5, 2, 5, nx, 1, nz), f32),
            pltpu.VMEM((5, 2, 5, nx, 1, nz), f32),
            pltpu.VMEM((5, 4, 1, nz), f32),
            pltpu.VMEM((5, 4, 1, nz), f32),
            pltpu.SemaphoreType.DMA((23,)),
            pltpu.SemaphoreType.DMA((5, 8)),
            pltpu.SemaphoreType.DMA((5, 8)),
        ],
        compiler_params=pltpu.CompilerParams(
            collective_id=0, has_side_effects=True, vmem_limit_bytes=44 * MIB
        ),
        name="forward",
    )(checkpoint, fluid, adjoint_in)
    return pl.pallas_call(
        write_kernel,
        out_shape=(jax.ShapeDtypeStruct((n, nx, ny, nz), f32),) * 2,
        in_specs=[pl.BlockSpec(memory_space=pltpu.VMEM)] * 2,
        out_specs=[pl.BlockSpec(memory_space=pl.ANY)] * 2,
        scratch_shapes=[pltpu.SemaphoreType.DMA((2, n))],
        compiler_params=pltpu.CompilerParams(vmem_limit_bytes=4 * MIB),
        name="write",
    )(state, adjoint)


def solution(mesh):
    return jax.shard_map(
        per_device,
        mesh=mesh,
        in_specs=(P(None, "gx", "gy", None), P("gx", "gy", None), P(None, "gx", "gy", None)),
        out_specs=(P(None, "gx", "gy", None), P(None, "gx", "gy", None)),
        check_vma=False,
    )
```

```python
import jax
import jax.numpy as jnp
from jax import lax
from jax.experimental import pallas as pl
from jax.experimental.pallas import tpu as pltpu
from jax.sharding import PartitionSpec as P

VELOCITY = [
    (0, 0, 0),
    (1, 0, 0),
    (-1, 0, 0),
    (0, 1, 0),
    (0, -1, 0),
    (0, 0, 1),
    (0, 0, -1),
    (1, 1, 0),
    (-1, -1, 0),
    (1, -1, 0),
    (-1, 1, 0),
    (1, 0, 1),
    (-1, 0, -1),
    (1, 0, -1),
    (-1, 0, 1),
    (0, 1, 1),
    (0, -1, -1),
    (0, 1, -1),
    (0, -1, 1),
]
OPPOSITE = [0, 2, 1, 4, 3, 6, 5, 8, 7, 10, 9, 12, 11, 14, 13, 16, 15, 18, 17]
ORDER = [0, 1, 7, 9, 11, 13, 2, 8, 10, 12, 14, 3, 4, 5, 6, 15, 16, 17, 18]
SLOT = [ORDER.index(q) for q in range(19)]
UP = [3, 7, 10, 15, 17]
DOWN = [4, 8, 9, 16, 18]
CORNER = [7, 8, 9, 10]
PAD = 8
T = 8
MIB = 1 << 20


def shifted(ref, q, x, y, speed):
    row = PAD + T * y - speed[1]
    tile = ref[SLOT[q], x + 1 - speed[0], row : row + T, :]
    if speed[2]:
        tile = pltpu.roll(tile, speed[2] % tile.shape[1], 1)
    return tile


def own(ref, q, x, y):
    return ref[SLOT[q], x + 1, PAD + T * y : PAD + T * y + T, :]


def stream(ref, bits, x, y):
    result = [own(ref, 0, x, y)]
    for q in range(1, 19):
        is_open = (bits & (1 << q)) != 0
        result.append(
            jnp.where(is_open, shifted(ref, q, x, y, VELOCITY[q]), own(ref, OPPOSITE[q], x, y))
        )
    return result


def moments(v):
    s = {q: v[q] + v[q + 1] for q in range(1, 19, 2)}
    d = {q: v[q] - v[q + 1] for q in range(1, 19, 2)}
    rho = v[0] + ((s[1] + s[3]) + (s[5] + s[7])) + ((s[9] + s[11]) + (s[13] + (s[15] + s[17])))
    mx = d[1] + (d[7] + d[9]) + (d[11] + d[13])
    my = d[3] + (d[7] - d[9]) + (d[15] + d[17])
    mz = d[5] + (d[11] - d[13]) + (d[15] - d[17])
    return rho, mx, my, mz


def collide(v):
    rho, mx, my, mz = moments(v)
    inverse = 3.0 / rho
    ux, uy, uz = mx * inverse, my * inverse, mz * inverse
    base = 1.0 - (ux * ux + uy * uy + uz * uz) * (1.0 / 6.0)
    along = {
        1: ux,
        3: uy,
        5: uz,
        7: ux + uy,
        9: ux - uy,
        11: ux + uz,
        13: ux - uz,
        15: uy + uz,
        17: uy - uz,
    }
    axis, diagonal = rho * (1.6 / 18.0), rho * (1.6 / 36.0)
    result = [rho * (1.6 / 3.0) * base - 0.6 * v[0]]
    for q in range(1, 19, 2):
        a = along[q]
        even = base + 0.5 * (a * a)
        factor = axis if q < 7 else diagonal
        result.append(factor * (even + a) - 0.6 * v[q])
        result.append(factor * (even - a) - 0.6 * v[q + 1])
    return result


def pull_back(v, b):
    rho, mx, my, mz = moments(v)
    inverse = 1.0 / rho
    ux, uy, uz = mx * inverse, my * inverse, mz * inverse
    s = {q: b[q] + b[q + 1] for q in range(1, 19, 2)}
    d = {q: b[q] - b[q + 1] for q in range(1, 19, 2)}
    for q in (1, 3, 5):
        s[q] = s[q] + s[q]
        d[q] = d[q] + d[q]
    sxy_p, sxz_p, syz_p = s[7] + s[9], s[11] + s[13], s[15] + s[17]
    sxy, sxz, syz = s[7] - s[9], s[11] - s[13], s[15] - s[17]
    s0 = 12.0 * b[0] + (s[1] + s[3]) + (s[5] + sxy_p) + (sxz_p + syz_p)
    sxx, syy, szz = s[1] + sxy_p + sxz_p, s[3] + sxy_p + syz_p, s[5] + sxz_p + syz_p
    s1x = d[1] + (d[7] + d[9]) + (d[11] + d[13])
    s1y = d[3] + (d[7] - d[9]) + (d[15] + d[17])
    s1z = d[5] + (d[11] - d[13]) + (d[15] - d[17])
    tx = sxx * ux + sxy * uy + sxz * uz
    ty = sxy * ux + syy * uy + syz * uz
    tz = sxz * ux + syz * uy + szz * uz
    k = 1.6 / 36.0
    square = ux * ux + uy * uy + uz * uz
    level = k * (s0 * (1.0 + 1.5 * square) - 4.5 * (ux * tx + uy * ty + uz * tz))
    gx = (3.0 * k) * (s1x + 3.0 * tx - ux * s0)
    gy = (3.0 * k) * (s1y + 3.0 * ty - uy * s0)
    gz = (3.0 * k) * (s1z + 3.0 * tz - uz * s0)
    along = {
        1: gx,
        3: gy,
        5: gz,
        7: gx + gy,
        9: gx - gy,
        11: gx + gz,
        13: gx - gz,
        15: gy + gz,
        17: gy - gz,
    }
    result = [level - 0.6 * b[0]]
    for q in range(1, 19, 2):
        result.append((level + along[q]) - 0.6 * b[q])
        result.append((level - along[q]) - 0.6 * b[q + 1])
    return result


def forward_kernel(
    start_ref, fluid_ref, seed_ref,
    state_ref, adjoint_ref,
    post_a, held, bits_ref, post_b, start, cells, solid, y_send, y_recv, c_send, c_recv,
    load_sem, send_sem, recv_sem, seed_send, seed_recv,
):
    _, nx, ny, nz = start_ref.shape
    tiles = ny // T
    last = tiles - 1
    top = PAD + ny
    me = {"gx": lax.axis_index("gx"), "gy": lax.axis_index("gy")}
    count = {"gx": lax.axis_size("gx"), "gy": lax.axis_size("gy")}

    def device(dx, dy):
        to_x = lax.rem(me["gx"] + dx + count["gx"], count["gx"])
        to_y = lax.rem(me["gy"] + dy + count["gy"], count["gy"])
        return (to_x, to_y)

    around = [(i, j) for i in (-1, 0, 1) for j in (-1, 0, 1) if (i, j) != (0, 0)]
    barrier = pltpu.get_barrier_semaphore()
    for i, j in around:
        pl.semaphore_signal(barrier, inc=1, device_id=device(i, j), device_id_type=pl.DeviceIdType.MESH)

    fluid_load = pltpu.make_async_copy(fluid_ref, cells, load_sem.at[0])
    fluid_load.start()
    start_load = [
        pltpu.make_async_copy(start_ref.at[:, pl.ds(a, n)], start.at[:, pl.ds(a, n)], load_sem.at[1 + i])
        for i, (a, n) in enumerate(((0, 1), (nx - 1, 1), (1, nx - 2)))
    ]
    for load in start_load:
        load.start()
    seed_load = [
        pltpu.make_async_copy(
            seed_ref.at[q],
            held.at[SLOT[OPPOSITE[q]], pl.ds(1, nx), pl.ds(PAD, ny)],
            load_sem.at[4 + q],
        )
        for q in range(19)
    ]
    pl.semaphore_wait(barrier, len(around))
    seed_faces = []
    for i, (plane, halo, first_slot) in enumerate(((nx - 1, 0, 1), (0, nx + 1, 6))):
        for k in range(5):
            slot = first_slot + k
            seed_faces.append(
                pltpu.make_async_remote_copy(
                    src_ref=seed_ref.at[OPPOSITE[ORDER[slot]], plane],
                    dst_ref=held.at[slot, halo, pl.ds(PAD, ny)],
                    send_sem=seed_send.at[i, k],
                    recv_sem=seed_recv.at[i, k],
                    device_id=device(1 - 2 * i, 0),
                    device_id_type=pl.DeviceIdType.MESH,
                )
            )
    for copy in seed_faces:
        copy.start()

    def copies(e, ref, is_cells, first_of=0):
        made = []
        for i, (plane, halo, first) in enumerate(((nx, 0, 1), (1, nx + 1, 6))):
            rows = pl.ds(PAD, ny)
            if is_cells:
                source, target = ref.at[plane, rows], ref.at[halo, rows]
            else:
                five = pl.ds(first, 5)
                source, target = ref.at[five, plane, rows], ref.at[five, halo, rows]
            made.append((source, target, device(1 - 2 * i, 0)))
        for i in range(2):
            made.append((y_send.at[e, i], y_recv.at[e, i], device(0, 1 - 2 * i)))
        for i, q in enumerate(CORNER):
            made.append((c_send.at[e, i], c_recv.at[e, i], device(VELOCITY[q][0], VELOCITY[q][1])))
        return [
            pltpu.make_async_remote_copy(
                src_ref=source, dst_ref=target, send_sem=send_sem.at[e, i], recv_sem=recv_sem.at[e, i],
                device_id=to, device_id_type=pl.DeviceIdType.MESH,
            )
            for i, (source, target, to) in enumerate(made)
            if i >= first_of
        ]

    def pack(e, ref):
        def one(x, _):
            for k in range(5):
                y_send[e, 0, k, x] = ref[SLOT[UP[k]], x + 1, top - 1 : top, :]
                y_send[e, 1, k, x] = ref[SLOT[DOWN[k]], x + 1, PAD : PAD + 1, :]
            return 0

        lax.fori_loop(0, nx, one, 0)
        for i, q in enumerate(CORNER):
            plane = nx if VELOCITY[q][0] == 1 else 1
            row = top - 1 if VELOCITY[q][1] == 1 else PAD
            c_send[e, i] = ref[SLOT[q], plane, row : row + 1, :]

    def unpack(e, ref):
        def one(x, _):
            for k in range(5):
                ref[SLOT[UP[k]], x + 1, PAD - 1 : PAD, :] = y_recv[e, 0, k, x]
                ref[SLOT[DOWN[k]], x + 1, top : top + 1, :] = y_recv[e, 1, k, x]
            return 0

        lax.fori_loop(0, nx, one, 0)
        for i, q in enumerate(CORNER):
            plane = 0 if VELOCITY[q][0] == 1 else nx + 1
            row = PAD - 1 if VELOCITY[q][1] == 1 else top
            ref[SLOT[q], plane, row : row + 1, :] = c_recv[e, i]

    def sweep_faces(body):
        def face(i, _):
            for y in range(tiles):
                body(i * (nx - 1), y)
            return 0

        lax.fori_loop(0, 2, face, 0)

    def sweep_edges(body):
        def edge(x, _):
            body(x, 0)
            body(x, last)
            return 0

        lax.fori_loop(1, nx - 1, edge, 0)

    def sweep_interior(body):
        def line(x, _):
            for y in range(1, last):
                body(x, y)
            return 0

        lax.fori_loop(1, nx - 1, line, 0)

    def begin(made):
        for copy in made:
            copy.start()

    def finish(made):
        for copy in made:
            copy.wait()

    fluid_load.wait()

    def to_float(x, _):
        solid[x + 1, PAD:top, :] = cells[x].astype(jnp.float32)
        y_send[0, 0, 0, x] = solid[x + 1, top - 1 : top, :]
        y_send[0, 1, 0, x] = solid[x + 1, PAD : PAD + 1, :]
        for k in range(1, 5):
            y_send[0, 0, k, x] = jnp.zeros((1, nz), jnp.float32)
            y_send[0, 1, k, x] = jnp.zeros((1, nz), jnp.float32)
        return 0

    lax.fori_loop(0, nx, to_float, 0)
    for i, q in enumerate(CORNER):
        plane = nx if VELOCITY[q][0] == 1 else 1
        row = top - 1 if VELOCITY[q][1] == 1 else PAD
        c_send[0, i] = solid[plane, row : row + 1, :]
    cell_copies = copies(0, solid, True)
    begin(cell_copies)

    def store(to, x, y, v, is_fluid):
        for q, value in enumerate(collide(v)):
            to[SLOT[q], x + 1, PAD + T * y : PAD + T * y + T, :] = jnp.where(
                is_fluid, value, v[OPPOSITE[q]]
            )

    def first(x, y):
        v = [start[q, x, T * y : T * y + T, :] for q in range(19)]
        store(post_a, x, y, v, solid[x + 1, PAD + T * y : PAD + T * y + T, :] > 0.5)

    for load in start_load[:2]:
        load.wait()
    first_copies = copies(1, post_a, False)
    sweep_faces(first)
    begin(first_copies[:2])
    start_load[2].wait()
    for load in seed_load:
        load.start()
    sweep_edges(first)
    pack(1, post_a)
    begin(first_copies[2:])
    sweep_interior(first)

    for load in seed_load:
        load.wait()
    pack(4, held)
    seed_copies = copies(4, held, False, 2)
    begin(seed_copies)

    finish(cell_copies)

    def place_cells(x, _):
        solid[x + 1, PAD - 1 : PAD, :] = y_recv[0, 0, 0, x]
        solid[x + 1, top : top + 1, :] = y_recv[0, 1, 0, x]
        return 0

    lax.fori_loop(0, nx, place_cells, 0)
    for i, q in enumerate(CORNER):
        plane = 0 if VELOCITY[q][0] == 1 else nx + 1
        row = PAD - 1 if VELOCITY[q][1] == 1 else top
        solid[plane, row : row + 1, :] = c_recv[0, i]

    layer = lax.broadcasted_iota(jnp.int32, (T, nz), 1)
    inside = {1: (layer > 0).astype(jnp.float32), -1: (layer < nz - 1).astype(jnp.float32)}

    def mark(x, _):
        for y in range(tiles):
            flat, up, down = 1.0, 0.0, 0.0
            for q in range(1, 19):
                c = VELOCITY[q]
                row = PAD + T * y - c[1]
                tile = solid[x + 1 - c[0], row : row + T, :] * float(1 << q)
                if c[2] == 0:
                    flat = flat + tile
                elif c[2] == 1:
                    up = up + tile
                else:
                    down = down + tile
            total = flat + pltpu.roll(up, 1, 1) * inside[1] + pltpu.roll(down, nz - 1, 1) * inside[-1]
            here = solid[x + 1, PAD + T * y : PAD + T * y + T, :]
            bits_ref[x, T * y : T * y + T, :] = (total * here).astype(jnp.int32)
        return 0

    lax.fori_loop(0, nx, mark, 0)

    def middle(source, to):
        def body(x, y):
            bits = bits_ref[x, T * y : T * y + T, :]
            v = stream(source, bits, x, y)
            store(to, x, y, v, (bits & 1) != 0)

        return body

    def step(e, made, source, to):
        body = middle(source, to)
        sweep_interior(body)
        finish(made[2:])
        unpack(e, source)
        sweep_edges(body)
        finish(made[:2])
        sweep_faces(body)
        later = copies(e + 1, to, False)
        begin(later[:2])
        pack(e + 1, to)
        begin(later[2:])
        return later

    second_copies = step(1, first_copies, post_a, post_b)
    third_copies = step(2, second_copies, post_b, post_a)
    finish(seed_copies)
    unpack(4, held)

    def final(x, y):
        rows = slice(T * y, T * y + T)
        bits = bits_ref[x, rows, :]
        v = stream(post_a, bits, x, y)
        for q in range(19):
            state_ref[q, x, rows, :] = v[q]
        turned = stream(held, bits, x, y)
        through = pull_back(v, [turned[OPPOSITE[q]] for q in range(19)])
        is_fluid = (bits & 1) != 0
        for q in range(19):
            adjoint_ref[q, x, rows, :] = jnp.where(is_fluid, through[q], turned[q])

    sweep_interior(final)
    finish(third_copies[2:])
    unpack(3, post_a)
    sweep_edges(final)
    finish(third_copies[:2])
    finish(seed_faces)
    sweep_faces(final)


def write_kernel(state_in, adjoint_in, state_ref, adjoint_ref, sem):
    made = []
    for i, (source, target) in enumerate(((state_in, state_ref), (adjoint_in, adjoint_ref))):
        for q in range(source.shape[0]):
            made.append(pltpu.make_async_copy(source.at[q], target.at[q], sem.at[i, q]))
    for copy in made:
        copy.start()
    for copy in made:
        copy.wait()


def per_device(checkpoint, fluid, adjoint_in):
    n, nx, ny, nz = checkpoint.shape
    padded = (n, nx + 2, ny + 2 * PAD, nz)
    f32 = jnp.float32
    state, adjoint = pl.pallas_call(
        forward_kernel,
        out_shape=(
            pltpu.VMEM((n, nx, ny, nz), f32),
            pltpu.VMEM((n, nx, ny, nz), f32),
        ),
        in_specs=[pl.BlockSpec(memory_space=pltpu.HBM)] * 3,
        out_specs=[pl.BlockSpec(memory_space=pltpu.VMEM)] * 2,
        scratch_shapes=[
            pltpu.VMEM(padded, f32),
            pltpu.VMEM(padded, f32),
            pltpu.VMEM((nx, ny, nz), jnp.int32),
            pltpu.VMEM(padded, f32),
            pltpu.VMEM((n, nx, ny, nz), f32),
            pltpu.VMEM((nx, ny, nz), jnp.int32),
            pltpu.VMEM(padded[1:], f32),
            pltpu.VMEM((5, 2, 5, nx, 1, nz), f32),
            pltpu.VMEM((5, 2, 5, nx, 1, nz), f32),
            pltpu.VMEM((5, 4, 1, nz), f32),
            pltpu.VMEM((5, 4, 1, nz), f32),
            pltpu.SemaphoreType.DMA((23,)),
            pltpu.SemaphoreType.DMA((5, 8)),
            pltpu.SemaphoreType.DMA((5, 8)),
            pltpu.SemaphoreType.DMA((2, 5)),
            pltpu.SemaphoreType.DMA((2, 5)),
        ],
        compiler_params=pltpu.CompilerParams(
            collective_id=0, has_side_effects=True, vmem_limit_bytes=50 * MIB
        ),
        name="forward",
    )(checkpoint, fluid, adjoint_in)
    return pl.pallas_call(
        write_kernel,
        out_shape=(jax.ShapeDtypeStruct((n, nx, ny, nz), f32),) * 2,
        in_specs=[pl.BlockSpec(memory_space=pltpu.VMEM)] * 2,
        out_specs=[pl.BlockSpec(memory_space=pl.ANY)] * 2,
        scratch_shapes=[pltpu.SemaphoreType.DMA((2, n))],
        compiler_params=pltpu.CompilerParams(vmem_limit_bytes=4 * MIB),
        name="write",
    )(state, adjoint)


def solution(mesh):
    return jax.shard_map(
        per_device,
        mesh=mesh,
        in_specs=(P(None, "gx", "gy", None), P("gx", "gy", None), P(None, "gx", "gy", None)),
        out_specs=(P(None, "gx", "gy", None), P(None, "gx", "gy", None)),
        check_vma=False,
    )
```

```python
import jax
import jax.numpy as jnp
from jax import lax
from jax.experimental import pallas as pl
from jax.experimental.pallas import tpu as pltpu
from jax.sharding import PartitionSpec as P

VELOCITY = [
    (0, 0, 0),
    (1, 0, 0),
    (-1, 0, 0),
    (0, 1, 0),
    (0, -1, 0),
    (0, 0, 1),
    (0, 0, -1),
    (1, 1, 0),
    (-1, -1, 0),
    (1, -1, 0),
    (-1, 1, 0),
    (1, 0, 1),
    (-1, 0, -1),
    (1, 0, -1),
    (-1, 0, 1),
    (0, 1, 1),
    (0, -1, -1),
    (0, 1, -1),
    (0, -1, 1),
]
OPPOSITE = [0, 2, 1, 4, 3, 6, 5, 8, 7, 10, 9, 12, 11, 14, 13, 16, 15, 18, 17]
ORDER = [0, 1, 7, 9, 11, 13, 2, 8, 10, 12, 14, 3, 4, 5, 6, 15, 16, 17, 18]
SLOT = [ORDER.index(q) for q in range(19)]
UP = [3, 7, 10, 15, 17]
DOWN = [4, 8, 9, 16, 18]
CORNER = [7, 8, 9, 10]
PAD = 8
T = 8
MIB = 1 << 20


def shifted(ref, q, x, y, speed):
    row = PAD + T * y - speed[1]
    tile = ref[SLOT[q], x + 1 - speed[0], row : row + T, :]
    if speed[2]:
        tile = pltpu.roll(tile, speed[2] % tile.shape[1], 1)
    return tile


def own(ref, q, x, y):
    return ref[SLOT[q], x + 1, PAD + T * y : PAD + T * y + T, :]


def stream(ref, bits, x, y):
    result = [own(ref, 0, x, y)]
    for q in range(1, 19):
        is_open = (bits & (1 << q)) != 0
        result.append(
            jnp.where(is_open, shifted(ref, q, x, y, VELOCITY[q]), own(ref, OPPOSITE[q], x, y))
        )
    return result


def moments(v):
    s = {q: v[q] + v[q + 1] for q in range(1, 19, 2)}
    d = {q: v[q] - v[q + 1] for q in range(1, 19, 2)}
    rho = v[0] + ((s[1] + s[3]) + (s[5] + s[7])) + ((s[9] + s[11]) + (s[13] + (s[15] + s[17])))
    mx = d[1] + (d[7] + d[9]) + (d[11] + d[13])
    my = d[3] + (d[7] - d[9]) + (d[15] + d[17])
    mz = d[5] + (d[11] - d[13]) + (d[15] - d[17])
    return rho, mx, my, mz


def collide(v):
    rho, mx, my, mz = moments(v)
    inverse = 3.0 / rho
    ux, uy, uz = mx * inverse, my * inverse, mz * inverse
    base = 1.0 - (ux * ux + uy * uy + uz * uz) * (1.0 / 6.0)
    along = {
        1: ux,
        3: uy,
        5: uz,
        7: ux + uy,
        9: ux - uy,
        11: ux + uz,
        13: ux - uz,
        15: uy + uz,
        17: uy - uz,
    }
    axis, diagonal = rho * (1.6 / 18.0), rho * (1.6 / 36.0)
    result = [rho * (1.6 / 3.0) * base - 0.6 * v[0]]
    for q in range(1, 19, 2):
        a = along[q]
        even = base + 0.5 * (a * a)
        factor = axis if q < 7 else diagonal
        result.append(factor * (even + a) - 0.6 * v[q])
        result.append(factor * (even - a) - 0.6 * v[q + 1])
    return result


def pull_back(v, b):
    rho, mx, my, mz = moments(v)
    inverse = 1.0 / rho
    ux, uy, uz = mx * inverse, my * inverse, mz * inverse
    s = {q: b[q] + b[q + 1] for q in range(1, 19, 2)}
    d = {q: b[q] - b[q + 1] for q in range(1, 19, 2)}
    for q in (1, 3, 5):
        s[q] = s[q] + s[q]
        d[q] = d[q] + d[q]
    sxy_p, sxz_p, syz_p = s[7] + s[9], s[11] + s[13], s[15] + s[17]
    sxy, sxz, syz = s[7] - s[9], s[11] - s[13], s[15] - s[17]
    s0 = 12.0 * b[0] + (s[1] + s[3]) + (s[5] + sxy_p) + (sxz_p + syz_p)
    sxx, syy, szz = s[1] + sxy_p + sxz_p, s[3] + sxy_p + syz_p, s[5] + sxz_p + syz_p
    s1x = d[1] + (d[7] + d[9]) + (d[11] + d[13])
    s1y = d[3] + (d[7] - d[9]) + (d[15] + d[17])
    s1z = d[5] + (d[11] - d[13]) + (d[15] - d[17])
    tx = sxx * ux + sxy * uy + sxz * uz
    ty = sxy * ux + syy * uy + syz * uz
    tz = sxz * ux + syz * uy + szz * uz
    k = 1.6 / 36.0
    square = ux * ux + uy * uy + uz * uz
    level = k * (s0 * (1.0 + 1.5 * square) - 4.5 * (ux * tx + uy * ty + uz * tz))
    gx = (3.0 * k) * (s1x + 3.0 * tx - ux * s0)
    gy = (3.0 * k) * (s1y + 3.0 * ty - uy * s0)
    gz = (3.0 * k) * (s1z + 3.0 * tz - uz * s0)
    along = {
        1: gx,
        3: gy,
        5: gz,
        7: gx + gy,
        9: gx - gy,
        11: gx + gz,
        13: gx - gz,
        15: gy + gz,
        17: gy - gz,
    }
    result = [level - 0.6 * b[0]]
    for q in range(1, 19, 2):
        result.append((level + along[q]) - 0.6 * b[q])
        result.append((level - along[q]) - 0.6 * b[q + 1])
    return result


def forward_kernel(
    start_ref, fluid_ref, seed_ref,
    state_ref, adjoint_ref,
    post_a, held, bits_ref, post_b, start, cells, solid, y_send, y_recv, c_send, c_recv,
    load_sem, send_sem, recv_sem, seed_send, seed_recv,
):
    _, nx, ny, nz = start_ref.shape
    tiles = ny // T
    last = tiles - 1
    top = PAD + ny
    me = {"gx": lax.axis_index("gx"), "gy": lax.axis_index("gy")}
    count = {"gx": lax.axis_size("gx"), "gy": lax.axis_size("gy")}

    def device(dx, dy):
        to_x = lax.rem(me["gx"] + dx + count["gx"], count["gx"])
        to_y = lax.rem(me["gy"] + dy + count["gy"], count["gy"])
        return (to_x, to_y)

    around = [(i, j) for i in (-1, 0, 1) for j in (-1, 0, 1) if (i, j) != (0, 0)]
    barrier = pltpu.get_barrier_semaphore()
    for i, j in around:
        pl.semaphore_signal(barrier, inc=1, device_id=device(i, j), device_id_type=pl.DeviceIdType.MESH)

    fluid_load = pltpu.make_async_copy(fluid_ref, cells, load_sem.at[0])
    fluid_load.start()
    start_load = [
        pltpu.make_async_copy(start_ref.at[:, pl.ds(a, n)], start.at[:, pl.ds(a, n)], load_sem.at[1 + i])
        for i, (a, n) in enumerate(((0, 1), (nx - 1, 1), (1, nx - 2)))
    ]
    for load in start_load:
        load.start()
    seed_load = [
        pltpu.make_async_copy(
            seed_ref.at[q],
            held.at[SLOT[OPPOSITE[q]], pl.ds(1, nx), pl.ds(PAD, ny)],
            load_sem.at[4 + q],
        )
        for q in range(19)
    ]
    pl.semaphore_wait(barrier, len(around))
    seed_faces = []
    for i, (plane, halo, first_slot) in enumerate(((nx - 1, 0, 1), (0, nx + 1, 6))):
        for k in range(5):
            slot = first_slot + k
            seed_faces.append(
                pltpu.make_async_remote_copy(
                    src_ref=seed_ref.at[OPPOSITE[ORDER[slot]], plane],
                    dst_ref=held.at[slot, halo, pl.ds(PAD, ny)],
                    send_sem=seed_send.at[i, k],
                    recv_sem=seed_recv.at[i, k],
                    device_id=device(1 - 2 * i, 0),
                    device_id_type=pl.DeviceIdType.MESH,
                )
            )

    def copies(e, ref, is_cells, first_of=0):
        made = []
        for i, (plane, halo, first) in enumerate(((nx, 0, 1), (1, nx + 1, 6))):
            rows = pl.ds(PAD, ny)
            if is_cells:
                source, target = ref.at[plane, rows], ref.at[halo, rows]
            else:
                five = pl.ds(first, 5)
                source, target = ref.at[five, plane, rows], ref.at[five, halo, rows]
            made.append((source, target, device(1 - 2 * i, 0)))
        for i in range(2):
            made.append((y_send.at[e, i], y_recv.at[e, i], device(0, 1 - 2 * i)))
        for i, q in enumerate(CORNER):
            made.append((c_send.at[e, i], c_recv.at[e, i], device(VELOCITY[q][0], VELOCITY[q][1])))
        return [
            pltpu.make_async_remote_copy(
                src_ref=source, dst_ref=target, send_sem=send_sem.at[e, i], recv_sem=recv_sem.at[e, i],
                device_id=to, device_id_type=pl.DeviceIdType.MESH,
            )
            for i, (source, target, to) in enumerate(made)
            if i >= first_of
        ]

    def pack(e, ref):
        def one(x, _):
            for k in range(5):
                y_send[e, 0, k, x] = ref[SLOT[UP[k]], x + 1, top - 1 : top, :]
                y_send[e, 1, k, x] = ref[SLOT[DOWN[k]], x + 1, PAD : PAD + 1, :]
            return 0

        lax.fori_loop(0, nx, one, 0)
        for i, q in enumerate(CORNER):
            plane = nx if VELOCITY[q][0] == 1 else 1
            row = top - 1 if VELOCITY[q][1] == 1 else PAD
            c_send[e, i] = ref[SLOT[q], plane, row : row + 1, :]

    def unpack(e, ref):
        def one(x, _):
            for k in range(5):
                ref[SLOT[UP[k]], x + 1, PAD - 1 : PAD, :] = y_recv[e, 0, k, x]
                ref[SLOT[DOWN[k]], x + 1, top : top + 1, :] = y_recv[e, 1, k, x]
            return 0

        lax.fori_loop(0, nx, one, 0)
        for i, q in enumerate(CORNER):
            plane = 0 if VELOCITY[q][0] == 1 else nx + 1
            row = PAD - 1 if VELOCITY[q][1] == 1 else top
            ref[SLOT[q], plane, row : row + 1, :] = c_recv[e, i]

    def sweep_faces(body):
        def face(i, _):
            for y in range(tiles):
                body(i * (nx - 1), y)
            return 0

        lax.fori_loop(0, 2, face, 0)

    def sweep_edges(body):
        def edge(x, _):
            body(x, 0)
            body(x, last)
            return 0

        lax.fori_loop(1, nx - 1, edge, 0)

    def sweep_interior(body):
        def line(x, _):
            for y in range(1, last):
                body(x, y)
            return 0

        lax.fori_loop(1, nx - 1, line, 0)

    def begin(made):
        for copy in made:
            copy.start()

    def finish(made):
        for copy in made:
            copy.wait()

    fluid_load.wait()

    def to_float(x, _):
        solid[x + 1, PAD:top, :] = cells[x].astype(jnp.float32)
        y_send[0, 0, 0, x] = solid[x + 1, top - 1 : top, :]
        y_send[0, 1, 0, x] = solid[x + 1, PAD : PAD + 1, :]
        for k in range(1, 5):
            y_send[0, 0, k, x] = jnp.zeros((1, nz), jnp.float32)
            y_send[0, 1, k, x] = jnp.zeros((1, nz), jnp.float32)
        return 0

    lax.fori_loop(0, nx, to_float, 0)
    for i, q in enumerate(CORNER):
        plane = nx if VELOCITY[q][0] == 1 else 1
        row = top - 1 if VELOCITY[q][1] == 1 else PAD
        c_send[0, i] = solid[plane, row : row + 1, :]
    cell_copies = copies(0, solid, True)
    begin(cell_copies)

    def store(to, x, y, v, is_fluid):
        for q, value in enumerate(collide(v)):
            to[SLOT[q], x + 1, PAD + T * y : PAD + T * y + T, :] = jnp.where(
                is_fluid, value, v[OPPOSITE[q]]
            )

    def first(x, y):
        v = [start[q, x, T * y : T * y + T, :] for q in range(19)]
        store(post_a, x, y, v, solid[x + 1, PAD + T * y : PAD + T * y + T, :] > 0.5)

    for load in start_load[:2]:
        load.wait()
    first_copies = copies(1, post_a, False)
    sweep_faces(first)
    begin(first_copies[:2])
    start_load[2].wait()
    for load in seed_load:
        load.start()
    sweep_edges(first)
    pack(1, post_a)
    begin(first_copies[2:])
    sweep_interior(first)

    for load in seed_load:
        load.wait()
    pack(4, held)
    seed_copies = copies(4, held, False, 2)
    begin(seed_copies)
    for copy in seed_faces:
        copy.start()

    finish(cell_copies)

    def place_cells(x, _):
        solid[x + 1, PAD - 1 : PAD, :] = y_recv[0, 0, 0, x]
        solid[x + 1, top : top + 1, :] = y_recv[0, 1, 0, x]
        return 0

    lax.fori_loop(0, nx, place_cells, 0)
    for i, q in enumerate(CORNER):
        plane = 0 if VELOCITY[q][0] == 1 else nx + 1
        row = PAD - 1 if VELOCITY[q][1] == 1 else top
        solid[plane, row : row + 1, :] = c_recv[0, i]

    layer = lax.broadcasted_iota(jnp.int32, (T, nz), 1)
    inside = {1: (layer > 0).astype(jnp.float32), -1: (layer < nz - 1).astype(jnp.float32)}

    def mark(x, _):
        for y in range(tiles):
            flat, up, down = 1.0, 0.0, 0.0
            for q in range(1, 19):
                c = VELOCITY[q]
                row = PAD + T * y - c[1]
                tile = solid[x + 1 - c[0], row : row + T, :] * float(1 << q)
                if c[2] == 0:
                    flat = flat + tile
                elif c[2] == 1:
                    up = up + tile
                else:
                    down = down + tile
            total = flat + pltpu.roll(up, 1, 1) * inside[1] + pltpu.roll(down, nz - 1, 1) * inside[-1]
            here = solid[x + 1, PAD + T * y : PAD + T * y + T, :]
            bits_ref[x, T * y : T * y + T, :] = (total * here).astype(jnp.int32)
        return 0

    lax.fori_loop(0, nx, mark, 0)

    def middle(source, to):
        def body(x, y):
            bits = bits_ref[x, T * y : T * y + T, :]
            v = stream(source, bits, x, y)
            store(to, x, y, v, (bits & 1) != 0)

        return body

    def step(e, made, source, to):
        body = middle(source, to)
        sweep_interior(body)
        finish(made[2:])
        unpack(e, source)
        sweep_edges(body)
        finish(made[:2])
        sweep_faces(body)
        later = copies(e + 1, to, False)
        begin(later[:2])
        pack(e + 1, to)
        begin(later[2:])
        return later

    second_copies = step(1, first_copies, post_a, post_b)
    third_copies = step(2, second_copies, post_b, post_a)
    finish(seed_copies)
    unpack(4, held)

    def final(x, y):
        rows = slice(T * y, T * y + T)
        bits = bits_ref[x, rows, :]
        v = stream(post_a, bits, x, y)
        for q in range(19):
            state_ref[q, x, rows, :] = v[q]
        turned = stream(held, bits, x, y)
        through = pull_back(v, [turned[OPPOSITE[q]] for q in range(19)])
        is_fluid = (bits & 1) != 0
        for q in range(19):
            adjoint_ref[q, x, rows, :] = jnp.where(is_fluid, through[q], turned[q])

    sweep_interior(final)
    finish(third_copies[2:])
    unpack(3, post_a)
    sweep_edges(final)
    finish(third_copies[:2])
    finish(seed_faces)
    sweep_faces(final)


def write_kernel(state_in, adjoint_in, state_ref, adjoint_ref, sem):
    made = []
    for i, (source, target) in enumerate(((state_in, state_ref), (adjoint_in, adjoint_ref))):
        for q in range(source.shape[0]):
            made.append(pltpu.make_async_copy(source.at[q], target.at[q], sem.at[i, q]))
    for copy in made:
        copy.start()
    for copy in made:
        copy.wait()


def per_device(checkpoint, fluid, adjoint_in):
    n, nx, ny, nz = checkpoint.shape
    padded = (n, nx + 2, ny + 2 * PAD, nz)
    f32 = jnp.float32
    state, adjoint = pl.pallas_call(
        forward_kernel,
        out_shape=(
            pltpu.VMEM((n, nx, ny, nz), f32),
            pltpu.VMEM((n, nx, ny, nz), f32),
        ),
        in_specs=[pl.BlockSpec(memory_space=pltpu.HBM)] * 3,
        out_specs=[pl.BlockSpec(memory_space=pltpu.VMEM)] * 2,
        scratch_shapes=[
            pltpu.VMEM(padded, f32),
            pltpu.VMEM(padded, f32),
            pltpu.VMEM((nx, ny, nz), jnp.int32),
            pltpu.VMEM(padded, f32),
            pltpu.VMEM((n, nx, ny, nz), f32),
            pltpu.VMEM((nx, ny, nz), jnp.int32),
            pltpu.VMEM(padded[1:], f32),
            pltpu.VMEM((5, 2, 5, nx, 1, nz), f32),
            pltpu.VMEM((5, 2, 5, nx, 1, nz), f32),
            pltpu.VMEM((5, 4, 1, nz), f32),
            pltpu.VMEM((5, 4, 1, nz), f32),
            pltpu.SemaphoreType.DMA((23,)),
            pltpu.SemaphoreType.DMA((5, 8)),
            pltpu.SemaphoreType.DMA((5, 8)),
            pltpu.SemaphoreType.DMA((2, 5)),
            pltpu.SemaphoreType.DMA((2, 5)),
        ],
        compiler_params=pltpu.CompilerParams(
            collective_id=0, has_side_effects=True, vmem_limit_bytes=50 * MIB
        ),
        name="forward",
    )(checkpoint, fluid, adjoint_in)
    return pl.pallas_call(
        write_kernel,
        out_shape=(jax.ShapeDtypeStruct((n, nx, ny, nz), f32),) * 2,
        in_specs=[pl.BlockSpec(memory_space=pltpu.VMEM)] * 2,
        out_specs=[pl.BlockSpec(memory_space=pl.ANY)] * 2,
        scratch_shapes=[pltpu.SemaphoreType.DMA((2, n))],
        compiler_params=pltpu.CompilerParams(vmem_limit_bytes=4 * MIB),
        name="write",
    )(state, adjoint)


def solution(mesh):
    return jax.shard_map(
        per_device,
        mesh=mesh,
        in_specs=(P(None, "gx", "gy", None), P("gx", "gy", None), P(None, "gx", "gy", None)),
        out_specs=(P(None, "gx", "gy", None), P(None, "gx", "gy", None)),
        check_vma=False,
    )
```
